512 devices in a mesh: fft: 16 (over z_lo, core), band: 32 (over z_hi, y, x).
Axes of the slice: x: 4, y: 4, z: 16 (z_hi: 2, z_lo: 8; z = z_hi * 8 + z_lo), core: 2. Of those that a mesh axis runs over, the one named last changes fastest.
Arguments:
- orbitals: float32 [2, 32, 3584, 128], P(None, 'band', 'fft'), may hold values from -6 to 6
- potential: float32 [128, 128, 128], P('fft'), may hold values from -6 to 6
- stick_coords: int32 [2, 3584], replicated, may hold values from -32 to 32, as said below
- stick_half: int32 [3584], replicated, may hold values from -1 to 32, as said below
Outputs:
- applied: float32 [2, 32, 3584, 128], P(None, 'band', 'fft')
- subspace: float32 [2, 2, 32, 32], replicated
The draws below stay inside these ranges and needn't reach their ends.
Inputs may be any that keep to these rules, and one draw needn't show every extreme that they name: `stick_coords`: the slots with stick_half >= 0 are exactly the columns (gx, gy) with gx**2 + gy**2 <= 32**2, each once, in an order drawn from the seed; the other slots have arbitrary coordinates in range. For a real stick, stick_half is the largest h with gx**2 + gy**2 + h**2 <= 32**2; empty slots hold -1.
All inputs are finite; a program needn't handle non-finite values.
Results may differ from the reference program's by a relative error of at most 0.0003.
Values may be sent and summed in bfloat16 or wider, within the bound.
No kernel may reach another device: no remote copies, remote signals or barrier semaphores. Data moves between devices by JAX's collectives and lax.ppermute only.
A program may use at most 128 MiB of HBM per device.

```python
import math
import jax
import jax.numpy as jnp
import numpy as np
from jax import lax

GRID = 128
RADIUS = 32
SLOTS = 128
STICKS = 3584
BANDS = 32


def sphere_table(key):
    entries = [(a, b, math.isqrt(RADIUS * RADIUS - a * a - b * b)) for a in range(-RADIUS, RADIUS + 1) for b in range(-RADIUS, RADIUS + 1) if a * a + b * b <= RADIUS * RADIUS]
    filled = jnp.asarray(np.array(entries, dtype=np.int32).T)
    spare = STICKS - filled.shape[1]
    loose_coords = jax.random.randint(jax.random.fold_in(key, 11), (2, spare), -RADIUS, RADIUS + 1).astype(jnp.int32)
    loose = jnp.concatenate([loose_coords, jnp.full((1, spare), -1, jnp.int32)], axis=0)
    table = jnp.concatenate([filled, loose], axis=1)
    order = jax.random.permutation(jax.random.fold_in(key, 12), STICKS)
    return table[:, order]


def draw_stick_coords(key, part):
    table = sphere_table(key)
    return table[:2]


def draw_stick_half(key, part):
    table = sphere_table(key)
    return table[2]


def steps_of(key, shape, pieces, smallest, largest):
    level = 1.0
    for axis_at, shards_of in pieces:
        draws = jax.random.uniform(jax.random.fold_in(jax.random.fold_in(key, 6), axis_at), (shards_of,), jnp.float32, smallest / len(pieces), largest / len(pieces))
        level = level * jnp.repeat(jnp.exp(draws), shape[axis_at] // shards_of).reshape((-1,) + (1,) * (len(shape) - 1 - axis_at))
    return level


def centred(rng, dims, scale, reach, split=(), kind=jnp.bfloat16):
    gain = steps_of(rng, dims, split, -0.22, 0.18) if split else 1.0
    values = jax.random.normal(rng, dims, jnp.float32) * scale * gain
    return jnp.minimum(jnp.maximum(values, -reach), reach).astype(kind)


def setup_inputs(seed: int = 0) -> dict:
    splits = jax.random.split(jax.random.key(seed), 5)
    return {
        "orbitals": centred(splits[0], (2, BANDS, STICKS, SLOTS), 1.0, 6.0, ((1, 32), (2, 16)), jnp.float32),
        "potential": centred(splits[1], (GRID, GRID, GRID), 1.0, 6.0, ((0, 16),), jnp.float32),
        "stick_coords": draw_stick_coords(jax.random.fold_in(splits[4], 71), 0),
        "stick_half": draw_stick_half(jax.random.fold_in(splits[4], 71), 0),
    }


def correlation_pair(first_set, second_set):
    formula = "bsk,csk->bc"
    real_sum = jnp.einsum(formula, first_set[0], second_set[0], precision=lax.Precision.HIGHEST) + jnp.einsum(formula, first_set[1], second_set[1], precision=lax.Precision.HIGHEST)
    imag_sum = jnp.einsum(formula, first_set[0], second_set[1], precision=lax.Precision.HIGHEST) - jnp.einsum(formula, first_set[1], second_set[0], precision=lax.Precision.HIGHEST)
    return jnp.stack([real_sum, imag_sum]) * (1.0 / (RADIUS ** 3))


def reference(orbitals, potential, stick_coords, stick_half):
    offsets = jnp.arange(SLOTS, dtype=jnp.int32) - RADIUS
    validity = (jnp.abs(offsets)[None, :] <= stick_half[:, None]).astype(jnp.float32)
    z_index = jnp.broadcast_to((offsets % GRID)[None, :], (STICKS, SLOTS)).astype(jnp.int32)
    x_index = jnp.broadcast_to((stick_coords[0] % GRID)[:, None], (STICKS, SLOTS)).astype(jnp.int32)
    y_index = jnp.broadcast_to((stick_coords[1] % GRID)[:, None], (STICKS, SLOTS)).astype(jnp.int32)
    squares = stick_coords[0][:, None] ** 2 + stick_coords[1][:, None] ** 2 + offsets[None, :] ** 2
    kinetic = squares.astype(jnp.float32) / (RADIUS * RADIUS)
    coeffs = orbitals * validity

    def apply_one(couple):
        values = couple[0] + 1j * couple[1]
        field = jnp.zeros((GRID, GRID, GRID), values.dtype).at[z_index, x_index, y_index].add(values)
        mixed = jnp.fft.fftn(potential * jnp.fft.ifftn(field))
        picked = mixed[z_index, x_index, y_index]
        return jnp.stack([jnp.real(picked), jnp.imag(picked)]).astype(jnp.float32)

    potential_part = lax.map(apply_one, jnp.moveaxis(coeffs, 1, 0))
    applied = (kinetic * coeffs + jnp.moveaxis(potential_part, 0, 1)) * validity
    left = lax.optimization_barrier(coeffs.astype(jnp.bfloat16)).astype(jnp.float32)
    right = lax.optimization_barrier(applied.astype(jnp.bfloat16)).astype(jnp.float32)
    subspace = jnp.stack([correlation_pair(left, right), correlation_pair(left, left)])
    return applied, subspace
```

```python
import math

import jax
import jax.numpy as jnp
import ml_dtypes
import numpy as np
from jax import lax
from jax.experimental import pallas as pl
from jax.experimental.pallas import tpu as pltpu
from jax.sharding import Mesh
from jax.sharding import PartitionSpec as P

RADIUS = 32
GRID = 128
SLOTS = 128
FFT = 16
OWN = 224
PAD = 256
PLANES = 8
GROUPS = 17
ROWS = GROUPS * 2 * PLANES
KX = 144
F32 = jnp.float32
BF16 = jnp.bfloat16
FULL = ("zlo", "core", "zhi", "y", "x")
VMEM = 48 * 1024 * 1024


def halves(table):
    high = table.astype(ml_dtypes.bfloat16)
    low = (table - high.astype(np.float64)).astype(ml_dtypes.bfloat16)
    return high, low


def waves(first, second):
    angle = (np.outer(first, second) % GRID) * (2.0 * math.pi / GRID)
    return np.cos(angle), np.sin(angle)


def z_table():
    cos, sin = waves(np.arange(GRID), np.arange(SLOTS) - RADIUS)
    cos[:, 2 * RADIUS + 1 :] = 0.0
    sin[:, 2 * RADIUS + 1 :] = 0.0
    real = np.concatenate([cos, -sin], axis=1).reshape(FFT, 1, PLANES, 2 * SLOTS)
    imag = np.concatenate([sin, cos], axis=1).reshape(FFT, 1, PLANES, 2 * SLOTS)
    return np.concatenate([real, imag], axis=1).reshape(2 * GRID, 2 * SLOTS)


def y_table():
    cos, sin = waves(np.arange(64) - RADIUS, np.arange(GRID))
    return np.tile(np.concatenate([cos, sin], axis=1), (4, 1))


def x_table():
    v = 4 * np.arange(GROUPS)[None, :] + np.arange(4)[:, None]
    freq = np.where(v <= 2 * RADIUS, v - RADIUS, 0).reshape(-1)
    cos, sin = waves(np.arange(GRID), freq)
    table = np.zeros((2 * GRID, KX))
    table[:GRID, :68], table[:GRID, 68:136] = cos, -sin
    table[GRID:, :68], table[GRID:, 68:136] = sin, cos
    return table


def y_back_table():
    cos, sin = waves(np.arange(GRID), np.arange(64) - RADIUS)
    real = np.concatenate([cos, sin], axis=0)
    imag = np.concatenate([-sin, cos], axis=0)
    return np.stack([np.tile(real, (1, 4)), np.tile(imag, (1, 4))]) * (1.0 / GRID**3)


def split(value):
    high = value.astype(BF16)
    return high, (value - high.astype(F32)).astype(BF16)


def dot(left, right):
    return jnp.dot(left, right, preferred_element_type=F32)


def dot3(left, right):
    return dot(left[0], right[0]) + dot(left[1], right[0]) + dot(left[0], right[1])


def masked(orbitals, rows):
    cols = jnp.transpose(rows)[:OWN]
    offset = lax.broadcasted_iota(jnp.int32, (OWN, SLOTS), 1).astype(F32) - RADIUS
    valid = jnp.abs(offset) <= cols[:, 0:1]
    real = jnp.where(valid, orbitals[0, 0], 0.0)
    imag = jnp.where(valid, orbitals[1, 0], 0.0)
    kinetic = (cols[:, 1:2] + offset * offset) * (1.0 / (RADIUS * RADIUS))
    return real, imag, valid, kinetic


def pack(real, imag):
    lane = lax.broadcasted_iota(jnp.int32, real.shape, 1)
    first = lane < 64
    main = jnp.where(first, real, pltpu.roll(imag, 64, 1))
    last = jnp.where(first, pltpu.roll(real, 64, 1), imag)
    last = jnp.where(lane % 64 == 0, last, 0.0)
    return main + jnp.concatenate([last[OWN - 1 :], last[: OWN - 1]], axis=0)


def z_kernel(orb_ref, rows_ref, high_ref, low_ref, out_ref, left_ref):
    real, imag, _, _ = masked(orb_ref, rows_ref[...])
    both = jnp.concatenate([real, imag], axis=1)
    both = jnp.concatenate([both, jnp.zeros((PAD - OWN, 2 * SLOTS), F32)], axis=0)
    high, low = split(both)
    contract = (((1,), (1,)), ((), ()))

    def product(a, b):
        return lax.dot_general(a, b, contract, preferred_element_type=F32)

    out = product(high_ref[...], high) + product(high_ref[...], low) + product(low_ref[...], high)
    out_ref[...] = out.reshape(FFT, 2 * PLANES, PAD)
    left_ref[...] = pack(real, imag).astype(BF16)


def plane_kernel(
    val_ref,
    group_ref,
    col_ref,
    colt_ref,
    pot_ref,
    yh_ref,
    yl_ref,
    xh_ref,
    xl_ref,
    bxh_ref,
    bxl_ref,
    byh_ref,
    byl_ref,
    out_ref,
    spread_ref,
    hot_ref,
    t_ref,
    g_ref,
):
    block = 2 * PLANES
    for c in range(FFT):
        value = val_ref[c]
        high = value.astype(BF16).astype(F32)
        low = value - high
        group = group_ref[c : c + 1, :]
        for r in range(GROUPS):
            here = jnp.broadcast_to(group == r, (block, PAD))
            spread_ref[r * block : (r + 1) * block, c * PAD : (c + 1) * PAD] = jnp.where(here, high, 0.0).astype(BF16)
            spread_ref[ROWS + r * block : ROWS + (r + 1) * block, c * PAD : (c + 1) * PAD] = jnp.where(here, low, 0.0).astype(BF16)
        lane = lax.broadcasted_iota(jnp.int32, (PAD, 256), 1)
        hot_ref[c * PAD : (c + 1) * PAD, :] = jnp.where(lane == colt_ref[:, c : c + 1], 1.0, 0.0).astype(BF16)
    window = dot(spread_ref[...], hot_ref[...])
    window = window[:ROWS] + window[ROWS:]

    quarter = lax.broadcasted_iota(jnp.int32, (ROWS, 256), 1) // 64
    stacked = jnp.concatenate([jnp.where(quarter == q, window, 0.0) for q in range(4)], axis=0)
    along = dot3(split(stacked), (yh_ref[...], yl_ref[...]))
    along = along.reshape(4, GROUPS, 2, PLANES, 256)
    real = along[:, :, 0, :, :GRID] - along[:, :, 1, :, GRID:]
    imag = along[:, :, 0, :, GRID:] + along[:, :, 1, :, :GRID]
    parity = lax.broadcasted_iota(jnp.int32, (PLANES, GRID), 1) % 2
    sign = jnp.where(parity == 1, -1.0, 1.0)
    half = 4 * GROUPS * PLANES
    t_ref[:half, :] = real.reshape(half, GRID)
    t_ref[half:, :] = imag.reshape(half, GRID)
    special = (GROUPS + 16) * PLANES
    for base in (special, half + special):
        t_ref[base : base + PLANES, :] = t_ref[base : base + PLANES, :] * sign

    count = 2 * 4 * GROUPS
    fill = jnp.zeros((KX - count, 256), F32)
    for pair in range(PLANES // 2):
        p = 2 * pair
        planes = [t_ref[pl.ds(p + i, count, stride=PLANES), :] for i in range(2)]
        part = jnp.concatenate([jnp.concatenate(planes, axis=1), fill], axis=0)
        field = dot3((xh_ref[...], xl_ref[...]), split(part))
        pot = jnp.concatenate([pot_ref[p], pot_ref[p + 1]], axis=1)
        field = field * jnp.concatenate([pot, pot], axis=0)
        back = dot3((bxh_ref[...], bxl_ref[...]), split(field))
        for i in range(2):
            g_ref[pl.ds(p + i, count, stride=PLANES), :] = back[:count, i * GRID : (i + 1) * GRID]
    for base in (special, half + special):
        g_ref[base : base + PLANES, :] = g_ref[base : base + PLANES, :] * sign

    couple = split(jnp.concatenate([g_ref[:half, :], g_ref[half:, :]], axis=1))
    parts = []
    rows = GROUPS * PLANES
    quarter = lax.broadcasted_iota(jnp.int32, (rows, 256), 1) // 64
    for i in range(2):
        cells = dot3(couple, (byh_ref[i], byl_ref[i]))
        total = jnp.zeros((rows, 256), F32)
        for q in range(4):
            total = jnp.where(quarter == q, cells[q * rows : (q + 1) * rows], total)
        parts.append(total.reshape(GROUPS, 1, PLANES, 256))
    cells = jnp.concatenate(parts, axis=1).reshape(ROWS, 256)
    high, low = split(cells)
    cells = jnp.concatenate([high, low], axis=0)

    sub = lax.broadcasted_iota(jnp.int32, (256, PAD), 0)
    for c in range(FFT):
        hot = jnp.where(sub == col_ref[c : c + 1, :], 1.0, 0.0).astype(BF16)
        found = dot(cells, hot)
        found = found[:ROWS] + found[ROWS:]
        group = group_ref[c : c + 1, :]
        total = jnp.zeros((block, PAD), F32)
        for r in range(GROUPS):
            here = jnp.broadcast_to(group == r, (block, PAD))
            total = jnp.where(here, found[r * block : (r + 1) * block], total)
        out_ref[c] = total


def apply_kernel(mix_ref, orb_ref, rows_ref, high_ref, low_ref, applied_ref, right_ref):
    real, imag, valid, kinetic = masked(orb_ref, rows_ref[...])
    mixed = dot3((high_ref[...], low_ref[...]), split(mix_ref[...].reshape(256, PAD)))
    mixed_real = jnp.transpose(mixed[:SLOTS])[:OWN]
    mixed_imag = jnp.transpose(mixed[SLOTS:])[:OWN]
    applied_real = jnp.where(valid, kinetic * real + mixed_real, 0.0)
    applied_imag = jnp.where(valid, kinetic * imag + mixed_imag, 0.0)
    applied_ref[0, 0] = applied_real
    applied_ref[1, 0] = applied_imag
    right_ref[...] = pack(applied_real, applied_imag).astype(BF16)


def column_kernel(all_ref, left_ref, right_ref, side_ref, out_ref, sums_ref, second_ref):
    groups, sides = all_ref.shape[0], all_ref.shape[1]
    bands = groups * sides
    lane = lax.broadcasted_iota(jnp.int32, (OWN, SLOTS), 1)
    sign = jnp.where(lane < 64, 1.0, -1.0)
    right = right_ref[...].astype(F32)
    left = left_ref[...].astype(F32)
    second_ref[0] = right
    second_ref[1] = pltpu.roll(right, 64, 1) * sign
    second_ref[2] = left
    second_ref[3] = pltpu.roll(left, 64, 1) * sign
    side = side_ref[0]
    for s in range(sides):
        def one(g, carry, s=s):
            row = ((side + s) % sides) * groups + g
            mine = all_ref[g, s].astype(F32)
            for t in range(4):
                product = (mine * second_ref[t]).reshape(OWN // 8, 8, SLOTS)
                sums_ref[pl.ds((t * bands + row) * 8, 8), :] = jnp.sum(product, axis=0)
            return carry

        lax.fori_loop(0, groups, one, 0)
    total = jnp.sum(sums_ref[...].reshape(4 * bands, 8, SLOTS), axis=1)
    ones = jnp.ones((8, SLOTS), F32)
    summed = lax.dot_general(
        ones, total, (((1,), (1,)), ((), ())), precision=lax.Precision.HIGHEST, preferred_element_type=F32
    )
    out_ref[...] = summed * (1.0 / RADIUS**3)


def call(kernel, out_shape, scratch=(), flops=10**8, smem=None, count=0):
    specs = [pl.BlockSpec(memory_space=pltpu.VMEM)] * count
    if smem is not None:
        specs[smem] = pl.BlockSpec(memory_space=pltpu.SMEM)
    return pl.pallas_call(
        kernel,
        out_shape=out_shape,
        in_specs=specs,
        scratch_shapes=list(scratch),
        compiler_params=pltpu.CompilerParams(vmem_limit_bytes=VMEM),
        cost_estimate=pl.CostEstimate(flops=flops, bytes_accessed=10**6, transcendentals=0),
    )


def solution(mesh):
    fft, band = mesh.shape["fft"], mesh.shape["band"]
    shape = (fft // 2, 2) + ((2, 4, 4) if band == 32 else (1, 1, band))
    fine = Mesh(mesh.devices.reshape(shape), FULL)
    sides, groups = shape[2], shape[3] * shape[4]
    bands = sides * groups
    shaped = jax.ShapeDtypeStruct

    zh, zl = halves(z_table())
    yh, yl = halves(y_table())
    xh, xl = halves(x_table())
    byh, byl = halves(y_back_table())

    def local(orbitals, potential, stick_coords, stick_half):
        me = lax.axis_index(("zlo", "core"))
        gx, gy = stick_coords[0], stick_coords[1]
        rows = jnp.stack([stick_half, gx * gx + gy * gy]).astype(F32)
        rows = lax.dynamic_slice_in_dim(rows, me * OWN, OWN, 1)
        rows = jnp.pad(rows, ((0, 6), (0, PAD - OWN)))

        sent, left = call(
            z_kernel,
            [shaped((FFT, 2 * PLANES, PAD), F32), shaped((OWN, SLOTS), BF16)],
            count=4,
        )(orbitals, rows, zh, zl)
        received = lax.all_to_all(sent, ("zlo", "core"), 0, 0, tiled=True)

        edge = gy == RADIUS
        v = jnp.where(edge, 2 * RADIUS + 1, gx + RADIUS)
        u = jnp.where(edge, 0, gy + RADIUS)
        group = jnp.where(stick_half >= 0, v // 4, -1)
        col = (v % 4) * 64 + u
        group = jnp.pad(group.reshape(FFT, OWN), ((0, 0), (0, PAD - OWN)), constant_values=-1)
        col = jnp.pad(col.reshape(FFT, OWN), ((0, 0), (0, PAD - OWN)))

        other = lax.ppermute(left, "zhi", [(i, (i + 1) % sides) for i in range(sides)]) if sides > 1 else None
        both = jnp.stack([left, other]) if sides > 1 else left[None]
        spread = jnp.broadcast_to(both[None], (groups,) + both.shape)
        everyone = lax.all_to_all(spread, ("y", "x"), 0, 0, tiled=True)

        picked = call(
            plane_kernel,
            shaped((FFT, 2 * PLANES, PAD), F32),
            scratch=[
                pltpu.VMEM((2 * ROWS, FFT * PAD), BF16),
                pltpu.VMEM((FFT * PAD, 256), BF16),
                pltpu.VMEM((2 * 4 * GROUPS * PLANES, GRID), F32),
                pltpu.VMEM((2 * 4 * GROUPS * PLANES, GRID), F32),
            ],
            flops=4 * 10**9,
            count=13,
        )(received, group, col, col.T, potential, yh, yl, xh, xl, xh.T, xl.T, byh, byl)
        mixed = lax.all_to_all(picked, ("zlo", "core"), 0, 0, tiled=True)
        applied, right = call(
            apply_kernel,
            [shaped(orbitals.shape, F32), shaped((OWN, SLOTS), BF16)],
            count=5,
        )(mixed, orbitals, rows, zh.T, zl.T)

        side = lax.axis_index("zhi").astype(jnp.int32).reshape(1)
        column = call(
            column_kernel,
            shaped((8, 4 * bands), F32),
            scratch=[pltpu.VMEM((4 * bands * 8, SLOTS), F32), pltpu.VMEM((4, OWN, SLOTS), F32)],
            smem=3,
            count=4,
        )(everyone, left, right, side)
        column = jnp.broadcast_to(column[:1][None], (fft * sides, 1, 4 * bands))
        column = lax.all_to_all(column, ("zlo", "core", "zhi"), 0, 0, tiled=True)
        column = jnp.sum(column.reshape(fft, sides, 4 * bands), axis=0)
        column = jnp.broadcast_to(column[None], (groups, sides, 4 * bands))
        columns = lax.all_to_all(column, ("y", "x"), 0, 0, tiled=True)
        columns = columns.reshape(groups, sides, 4, bands)
        subspace = jnp.transpose(columns, (2, 3, 1, 0)).reshape(2, 2, bands, bands)
        return applied, subspace

    across = ("zhi", "y", "x")
    along = ("zlo", "core")
    return jax.shard_map(
        local,
        mesh=fine,
        in_specs=(P(None, across, along, None), P(along, None, None), P(), P()),
        out_specs=(P(None, across, along, None), P()),
        check_vma=False,
    )
```

```python
import math

import jax
import jax.numpy as jnp
import ml_dtypes
import numpy as np
from jax import lax
from jax.experimental import pallas as pl
from jax.experimental.pallas import tpu as pltpu
from jax.sharding import Mesh
from jax.sharding import PartitionSpec as P

RADIUS = 32
GRID = 128
SLOTS = 128
FFT = 16
OWN = 224
PAD = 256
LEVELS = 32767.0
PLANES = 8
GROUPS = 17
ROWS = GROUPS * 2 * PLANES
KX = 144
F32 = jnp.float32
BF16 = jnp.bfloat16
FULL = ("zlo", "core", "zhi", "y", "x")
VMEM = 48 * 1024 * 1024


def halves(table):
    high = table.astype(ml_dtypes.bfloat16)
    low = (table - high.astype(np.float64)).astype(ml_dtypes.bfloat16)
    return high, low


def waves(first, second):
    angle = (np.outer(first, second) % GRID) * (2.0 * math.pi / GRID)
    return np.cos(angle), np.sin(angle)


def z_table():
    cos, sin = waves(np.arange(GRID), np.arange(SLOTS) - RADIUS)
    cos[:, 2 * RADIUS + 1 :] = 0.0
    sin[:, 2 * RADIUS + 1 :] = 0.0
    real = np.concatenate([cos, -sin], axis=1).reshape(FFT, 1, PLANES, 2 * SLOTS)
    imag = np.concatenate([sin, cos], axis=1).reshape(FFT, 1, PLANES, 2 * SLOTS)
    return np.concatenate([real, imag], axis=1).reshape(2 * GRID, 2 * SLOTS)


def y_table():
    cos, sin = waves(np.arange(64) - RADIUS, np.arange(GRID))
    return np.tile(np.concatenate([cos, sin], axis=1), (4, 1))


def x_table():
    v = 4 * np.arange(GROUPS)[None, :] + np.arange(4)[:, None]
    freq = np.where(v <= 2 * RADIUS, v - RADIUS, 0).reshape(-1)
    cos, sin = waves(np.arange(GRID), freq)
    table = np.zeros((2 * GRID, KX))
    table[:GRID, :68], table[:GRID, 68:136] = cos, -sin
    table[GRID:, :68], table[GRID:, 68:136] = sin, cos
    return table


def y_back_table():
    cos, sin = waves(np.arange(GRID), np.arange(64) - RADIUS)
    real = np.concatenate([cos, sin], axis=0)
    imag = np.concatenate([-sin, cos], axis=0)
    return np.stack([np.tile(real, (1, 4)), np.tile(imag, (1, 4))]) * (1.0 / GRID**3)


def split(value):
    high = value.astype(BF16)
    return high, (value - high.astype(F32)).astype(BF16)


def dot(left, right):
    return jnp.dot(left, right, preferred_element_type=F32)


def dot3(left, right):
    return dot(left[0], right[0]) + dot(left[1], right[0]) + dot(left[0], right[1])


def encode(value):
    top = jnp.max(jnp.max(jnp.abs(value), axis=1, keepdims=True), axis=2, keepdims=True)
    power = jnp.floor(jnp.log2(jnp.maximum(top, 1e-30))) + 1.0
    size = jnp.maximum(jnp.abs(value) * jnp.exp2(-power), 1e-30)
    size = jnp.minimum(jnp.exp2(jnp.log2(size) * (1.0 / 3.0)) * LEVELS + 0.5, LEVELS)
    size = jnp.floor(size)
    coded = jnp.where(value < 0.0, -size, size)
    lane = lax.broadcasted_iota(jnp.int32, value.shape, 2)
    return jnp.where(lane == OWN, power, coded).astype(jnp.int32).astype(jnp.int16)


def decode(coded):
    coded = coded.astype(jnp.int32).astype(F32)
    return coded * coded * coded * (jnp.exp2(coded[:, :, OWN : OWN + 1]) * (1.0 / LEVELS**3))


def masked(orbitals, cols):
    cols = cols[:OWN]
    offset = lax.broadcasted_iota(jnp.int32, (OWN, SLOTS), 1).astype(F32) - RADIUS
    valid = jnp.abs(offset) <= cols[:, 0:1]
    real = jnp.where(valid, orbitals[0, 0], 0.0)
    imag = jnp.where(valid, orbitals[1, 0], 0.0)
    kinetic = (cols[:, 1:2] + offset * offset) * (1.0 / (RADIUS * RADIUS))
    return real, imag, valid, kinetic


def pack(real, imag):
    lane = lax.broadcasted_iota(jnp.int32, real.shape, 1)
    first = lane < 64
    main = jnp.where(first, real, pltpu.roll(imag, 64, 1))
    last = jnp.where(first, pltpu.roll(real, 64, 1), imag)
    last = jnp.where(lane % 64 == 0, last, 0.0)
    return main + jnp.concatenate([last[OWN - 1 :], last[: OWN - 1]], axis=0)


def z_kernel(orb_hbm, high_hbm, low_hbm, coords_hbm, half_hbm, out_ref, left_ref, cols_ref, orb, high, low, coords, half, sems):
    pairs = ((half_hbm, half), (coords_hbm, coords), (orb_hbm, orb), (high_hbm, high), (low_hbm, low))
    copies = [pltpu.make_async_copy(a, b, sems.at[i]) for i, (a, b) in enumerate(pairs)]
    for copy in copies:
        copy.start()
    me = lax.axis_index("zlo") * 2 + lax.axis_index("core")
    tile = jnp.minimum(me * OWN // 128, 25)
    shift = me * OWN - tile * 128
    copies[0].wait()
    copies[1].wait()
    wide = pl.ds(pl.multiple_of(tile * 128, 128), 384)
    own = jnp.concatenate([half[pl.ds(tile + i, 1), :] for i in range(3)], axis=1)
    own = jnp.concatenate([own, coords[:, wide], jnp.zeros((5, 384), jnp.int32)], axis=0).astype(F32)
    own = pltpu.roll(own, lax.rem(384 - shift, 384), 1)[:, :PAD]
    squares = own[1:2] * own[1:2] + own[2:3] * own[2:3]
    cols = jnp.transpose(jnp.concatenate([own[:1], squares, own[2:]], axis=0))
    cols_ref[...] = cols
    copies[2].wait()
    real, imag, _, _ = masked(orb, cols)
    left = pack(real, imag).astype(BF16)
    left_ref[...] = left
    both = jnp.concatenate([real, imag], axis=1)
    both = split(jnp.concatenate([both, jnp.zeros((PAD - OWN, 2 * SLOTS), F32)], axis=0))
    contract = (((1,), (1,)), ((), ()))

    def product(a, b):
        return lax.dot_general(a, b, contract, preferred_element_type=F32)

    copies[3].wait()
    out = product(high[...], both[0]) + product(high[...], both[1])
    copies[4].wait()
    out = out + product(low[...], both[0])
    out_ref[...] = encode(out.reshape(FFT, 2 * PLANES, PAD))


def plane_kernel(
    val_ref,
    group_ref,
    col_ref,
    colt_ref,
    pot_ref,
    yh_ref,
    yl_ref,
    xh_ref,
    xl_ref,
    bxh_ref,
    bxl_ref,
    byh_ref,
    byl_ref,
    out_ref,
    spread_ref,
    hot_ref,
    t_ref,
    g_ref,
):
    block = 2 * PLANES
    values = decode(val_ref[...])
    for c in range(FFT):
        value = values[c]
        high = value.astype(BF16).astype(F32)
        low = value - high
        group = group_ref[c : c + 1, :]
        for r in range(GROUPS):
            here = jnp.broadcast_to(group == r, (block, PAD))
            spread_ref[r * block : (r + 1) * block, c * PAD : (c + 1) * PAD] = jnp.where(here, high, 0.0).astype(BF16)
            spread_ref[ROWS + r * block : ROWS + (r + 1) * block, c * PAD : (c + 1) * PAD] = jnp.where(here, low, 0.0).astype(BF16)
        lane = lax.broadcasted_iota(jnp.int32, (PAD, 256), 1)
        hot_ref[c * PAD : (c + 1) * PAD, :] = jnp.where(lane == colt_ref[:, c : c + 1], 1.0, 0.0).astype(BF16)
    window = dot(spread_ref[...], hot_ref[...])
    window = window[:ROWS] + window[ROWS:]

    quarter = lax.broadcasted_iota(jnp.int32, (ROWS, 256), 1) // 64
    stacked = jnp.concatenate([jnp.where(quarter == q, window, 0.0) for q in range(4)], axis=0)
    along = dot3(split(stacked), (yh_ref[...], yl_ref[...]))
    along = along.reshape(4, GROUPS, 2, PLANES, 256)
    real = along[:, :, 0, :, :GRID] - along[:, :, 1, :, GRID:]
    imag = along[:, :, 0, :, GRID:] + along[:, :, 1, :, :GRID]
    parity = lax.broadcasted_iota(jnp.int32, (PLANES, GRID), 1) % 2
    sign = jnp.where(parity == 1, -1.0, 1.0)
    half = 4 * GROUPS * PLANES
    t_ref[:half, :] = real.reshape(half, GRID)
    t_ref[half:, :] = imag.reshape(half, GRID)
    special = (GROUPS + 16) * PLANES
    for base in (special, half + special):
        t_ref[base : base + PLANES, :] = t_ref[base : base + PLANES, :] * sign

    count = 2 * 4 * GROUPS
    fill = jnp.zeros((KX - count, 256), F32)
    for pair in range(PLANES // 2):
        p = 2 * pair
        planes = [t_ref[pl.ds(p + i, count, stride=PLANES), :] for i in range(2)]
        part = jnp.concatenate([jnp.concatenate(planes, axis=1), fill], axis=0)
        field = dot3((xh_ref[...], xl_ref[...]), split(part))
        pot = jnp.concatenate([pot_ref[p], pot_ref[p + 1]], axis=1)
        field = field * jnp.concatenate([pot, pot], axis=0)
        back = dot3((bxh_ref[...], bxl_ref[...]), split(field))
        for i in range(2):
            g_ref[pl.ds(p + i, count, stride=PLANES), :] = back[:count, i * GRID : (i + 1) * GRID]
    for base in (special, half + special):
        g_ref[base : base + PLANES, :] = g_ref[base : base + PLANES, :] * sign

    couple = split(jnp.concatenate([g_ref[:half, :], g_ref[half:, :]], axis=1))
    parts = []
    rows = GROUPS * PLANES
    quarter = lax.broadcasted_iota(jnp.int32, (rows, 256), 1) // 64
    for i in range(2):
        cells = dot3(couple, (byh_ref[i], byl_ref[i]))
        total = jnp.zeros((rows, 256), F32)
        for q in range(4):
            total = jnp.where(quarter == q, cells[q * rows : (q + 1) * rows], total)
        parts.append(total.reshape(GROUPS, 1, PLANES, 256))
    cells = jnp.concatenate(parts, axis=1).reshape(ROWS, 256)
    high, low = split(cells)
    cells = jnp.concatenate([high, low], axis=0)

    sub = lax.broadcasted_iota(jnp.int32, (256, PAD), 0)
    for c in range(FFT):
        hot = jnp.where(sub == col_ref[c : c + 1, :], 1.0, 0.0).astype(BF16)
        found = dot(cells, hot)
        found = found[:ROWS] + found[ROWS:]
        group = group_ref[c : c + 1, :]
        total = jnp.zeros((block, PAD), F32)
        for r in range(GROUPS):
            here = jnp.broadcast_to(group == r, (block, PAD))
            total = jnp.where(here, found[r * block : (r + 1) * block], total)
        out_ref[c : c + 1] = encode(total[None])


def apply_kernel(mix_ref, orb_ref, cols_ref, high_ref, low_ref, applied_ref, spread_ref):
    real, imag, valid, kinetic = masked(orb_ref, cols_ref[...])
    mixed = dot3((high_ref[...], low_ref[...]), split(decode(mix_ref[...]).reshape(256, PAD)))
    mixed_real = jnp.transpose(mixed[:SLOTS])[:OWN]
    mixed_imag = jnp.transpose(mixed[SLOTS:])[:OWN]
    applied_real = jnp.where(valid, kinetic * real + mixed_real, 0.0)
    applied_imag = jnp.where(valid, kinetic * imag + mixed_imag, 0.0)
    applied_ref[0, 0] = applied_real
    applied_ref[1, 0] = applied_imag
    right = pack(applied_real, applied_imag).astype(BF16)
    left = pack(real, imag).astype(BF16)
    for i in range(spread_ref.shape[0]):
        spread_ref[i, 0] = right
        spread_ref[i, 1] = left


def block_kernel(left_ref, pair_ref, out_ref, sums_ref, second_ref):
    depth, sides = left_ref.shape[0], left_ref.shape[1]
    width = pair_ref.shape[0]
    lane = lax.broadcasted_iota(jnp.int32, (OWN, SLOTS), 1)
    sign = jnp.where(lane < 64, 1.0, -1.0)
    side, y = lax.axis_index("zhi"), lax.axis_index("y")

    def column(x, carry):
        for m in range(2):
            second = pair_ref[x, m].astype(F32)
            second_ref[2 * m] = second
            second_ref[2 * m + 1] = pltpu.roll(second, 64, 1) * sign

        def one(j, carry):
            order, other = j // sides, lax.rem(j, sides)
            mine = left_ref[order, other].astype(F32)
            flip = lax.rem(order, 2)
            near = y + flip * (1 - 2 * lax.rem(y, 2))
            row = jnp.where(order >= 2, depth - 1 - near, near) + depth * lax.rem(side + other, sides)
            for t in range(4):
                product = (mine * second_ref[t]).reshape(OWN // 8, 8, SLOTS)
                place = (t * sides * depth + row) * width + x
                sums_ref[pl.ds(pl.multiple_of(place * 8, 8), 8), :] = jnp.sum(product, axis=0)
            return carry

        return lax.fori_loop(0, depth * sides, one, carry)

    lax.fori_loop(0, width, column, 0)
    total = jnp.sum(sums_ref[...].reshape(-1, 8, SLOTS), axis=1)
    ones = jnp.ones((8, SLOTS), F32)
    summed = lax.dot_general(
        ones, total, (((1,), (1,)), ((), ())), precision=lax.Precision.HIGHEST, preferred_element_type=F32
    )
    out_ref[...] = summed * (1.0 / RADIUS**3)


def call(kernel, out_shape, count, scratch=(), flops=10**8, traffic=10**6, hbm=False, limit=VMEM):
    return pl.pallas_call(
        kernel,
        out_shape=out_shape,
        in_specs=[pl.BlockSpec(memory_space=pl.ANY if hbm else pltpu.VMEM)] * count,
        scratch_shapes=list(scratch),
        compiler_params=pltpu.CompilerParams(vmem_limit_bytes=limit),
        cost_estimate=pl.CostEstimate(flops=flops, bytes_accessed=traffic, transcendentals=0),
    )


def solution(mesh):
    fft, band = mesh.shape["fft"], mesh.shape["band"]
    shape = (fft // 2, 2) + ((2, 4, 4) if band == 32 else (1, 1, band))
    fine = Mesh(mesh.devices.reshape(shape), FULL)
    sides, depth, width = shape[2:]
    groups = depth * width
    bands = sides * groups
    shaped = jax.ShapeDtypeStruct

    zh, zl = halves(z_table())
    yh, yl = halves(y_table())
    xh, xl = halves(x_table())
    byh, byl = halves(y_back_table())

    def local(orbitals, potential, stick_coords, stick_half):
        gx, gy = stick_coords[0], stick_coords[1]
        stick = (OWN, SLOTS)
        sent, left, cols = call(
            z_kernel,
            [shaped((FFT, 2 * PLANES, PAD), jnp.int16), shaped(stick, BF16), shaped((PAD, 8), F32)],
            5,
            scratch=[
                pltpu.VMEM(orbitals.shape, F32),
                pltpu.VMEM(zh.shape, BF16),
                pltpu.VMEM(zl.shape, BF16),
                pltpu.VMEM(stick_coords.shape, jnp.int32),
                pltpu.VMEM((28, 128), jnp.int32),
                pltpu.SemaphoreType.DMA((5,)),
            ],
            hbm=True,
            limit=62 * 1024 * 1024,
        )(orbitals, zh, zl, stick_coords, stick_half.reshape(28, 128))
        received = lax.all_to_all(sent, ("zlo", "core"), 0, 0, tiled=True)

        edge = gy == RADIUS
        v = jnp.where(edge, 2 * RADIUS + 1, gx + RADIUS)
        u = jnp.where(edge, 0, gy + RADIUS)
        group = jnp.where(stick_half >= 0, v // 4, -1)
        col = (v % 4) * 64 + u
        group = jnp.pad(group.reshape(FFT, OWN), ((0, 0), (0, PAD - OWN)), constant_values=-1)
        col = jnp.pad(col.reshape(FFT, OWN), ((0, 0), (0, PAD - OWN)))

        picked = call(
            plane_kernel,
            shaped((FFT, 2 * PLANES, PAD), jnp.int16),
            13,
            scratch=[
                pltpu.VMEM((2 * ROWS, FFT * PAD), BF16),
                pltpu.VMEM((FFT * PAD, 256), BF16),
                pltpu.VMEM((2 * 4 * GROUPS * PLANES, GRID), F32),
                pltpu.VMEM((2 * 4 * GROUPS * PLANES, GRID), F32),
            ],
            flops=1,
            traffic=1,
        )(received, group, col, col.T, potential, yh, yl, xh, xl, xh.T, xl.T, byh, byl)
        lefts = left[None]
        if sides > 1:
            far = lax.ppermute(left, "zhi", [(0, 1), (1, 0)])
            picked, far = lax.optimization_barrier((picked, far))
            lefts = jnp.stack([left, far])
        lefts = lefts[None]
        if depth > 1:
            lefts = jnp.concatenate([lefts, lax.ppermute(lefts, "y", [(i, i ^ 1) for i in range(depth)])])
            lefts = jnp.concatenate([lefts, lax.ppermute(lefts, "y", [(i, depth - 1 - i) for i in range(depth)])])

        mixed = lax.all_to_all(picked, ("zlo", "core"), 0, 0, tiled=True)
        applied, spread = call(apply_kernel, [shaped(orbitals.shape, F32), shaped((width, 2) + stick, BF16)], 5)(
            mixed, orbitals, cols, zh.T, zl.T
        )
        pairs = lax.all_to_all(spread, "x", 0, 0, tiled=True)
        column = call(
            block_kernel,
            shaped((8, 4 * bands), F32),
            2,
            scratch=[pltpu.VMEM((4 * bands * 8, SLOTS), F32), pltpu.VMEM((4,) + stick, F32)],
        )(lefts, pairs)
        column = jnp.broadcast_to(column[:1][None], (fft * sides, 1, 4 * bands))
        column = lax.all_to_all(column, ("zlo", "core", "zhi"), 0, 0, tiled=True)
        column = jnp.sum(column.reshape(fft, sides, 4 * bands), axis=0)
        column = jnp.broadcast_to(column[None], (groups, sides, 4 * bands))
        columns = lax.all_to_all(column, ("y", "x"), 0, 0, tiled=True)
        columns = columns.reshape(depth, width, sides, 4, sides, depth, width)
        subspace = jnp.transpose(columns, (3, 4, 5, 1, 2, 0, 6)).reshape(2, 2, bands, bands)
        return applied, subspace

    across = ("zhi", "y", "x")
    along = ("zlo", "core")
    return jax.shard_map(
        local,
        mesh=fine,
        in_specs=(P(None, across, along, None), P(along, None, None), P(), P()),
        out_specs=(P(None, across, along, None), P()),
        check_vma=False,
    )
```

```python
import math

import jax
import jax.numpy as jnp
import ml_dtypes
import numpy as np
from jax import lax
from jax.experimental import pallas as pl
from jax.experimental.pallas import tpu as pltpu
from jax.sharding import Mesh
from jax.sharding import PartitionSpec as P

RADIUS = 32
GRID = 128
SLOTS = 128
FFT = 16
OWN = 224
PAD = 256
LEVELS = 32767.0
PLANES = 8
GROUPS = 17
ROWS = GROUPS * 2 * PLANES
KX = 144
F32 = jnp.float32
BF16 = jnp.bfloat16
FULL = ("zlo", "core", "zhi", "y", "x")
VMEM = 48 * 1024 * 1024
WHOLE = 62 * 1024 * 1024


def halves(table):
    high = table.astype(ml_dtypes.bfloat16)
    low = (table - high.astype(np.float64)).astype(ml_dtypes.bfloat16)
    return high, low


def waves(first, second):
    angle = (np.outer(first, second) % GRID) * (2.0 * math.pi / GRID)
    return np.cos(angle), np.sin(angle)


def z_table():
    cos, sin = waves(np.arange(GRID), np.arange(SLOTS) - RADIUS)
    cos[:, 2 * RADIUS + 1 :] = 0.0
    sin[:, 2 * RADIUS + 1 :] = 0.0
    real = np.concatenate([cos, -sin], axis=1).reshape(FFT, 1, PLANES, 2 * SLOTS)
    imag = np.concatenate([sin, cos], axis=1).reshape(FFT, 1, PLANES, 2 * SLOTS)
    return np.concatenate([real, imag], axis=1).reshape(2 * GRID, 2 * SLOTS)


def y_table():
    cos, sin = waves(np.arange(64) - RADIUS, np.arange(GRID))
    return np.tile(np.concatenate([cos, sin], axis=1), (4, 1))


def x_table():
    v = 4 * np.arange(GROUPS)[None, :] + np.arange(4)[:, None]
    freq = np.where(v <= 2 * RADIUS, v - RADIUS, 0).reshape(-1)
    cos, sin = waves(np.arange(GRID), freq)
    table = np.zeros((2 * GRID, KX))
    table[:GRID, :68], table[:GRID, 68:136] = cos, -sin
    table[GRID:, :68], table[GRID:, 68:136] = sin, cos
    return table


def y_back_table():
    cos, sin = waves(np.arange(GRID), np.arange(64) - RADIUS)
    real = np.concatenate([cos, sin], axis=0)
    imag = np.concatenate([-sin, cos], axis=0)
    return np.stack([np.tile(real, (1, 4)), np.tile(imag, (1, 4))]) * (1.0 / GRID**3)


def split(value):
    high = value.astype(BF16)
    return high, (value - high.astype(F32)).astype(BF16)


def dot(left, right):
    return jnp.dot(left, right, preferred_element_type=F32)


def dot3(left, right):
    return dot(left[0], right[0]) + dot(left[1], right[0]) + dot(left[0], right[1])


def encode(value):
    top = jnp.max(jnp.max(jnp.abs(value), axis=1, keepdims=True), axis=2, keepdims=True)
    power = jnp.floor(jnp.log2(jnp.maximum(top, 1e-30))) + 1.0
    size = jnp.maximum(jnp.abs(value) * jnp.exp2(-power), 1e-30)
    size = jnp.minimum(jnp.exp2(jnp.log2(size) * (1.0 / 3.0)) * LEVELS + 0.5, LEVELS)
    size = jnp.floor(size)
    coded = jnp.where(value < 0.0, -size, size)
    lane = lax.broadcasted_iota(jnp.int32, value.shape, 2)
    return jnp.where(lane == OWN, power, coded).astype(jnp.int32).astype(jnp.int16)


def decode(coded):
    coded = coded.astype(jnp.int32).astype(F32)
    return coded * coded * coded * (jnp.exp2(coded[:, :, OWN : OWN + 1]) * (1.0 / LEVELS**3))


def masked(orbitals, cols):
    cols = cols[:OWN]
    offset = lax.broadcasted_iota(jnp.int32, (OWN, SLOTS), 1).astype(F32) - RADIUS
    valid = jnp.abs(offset) <= cols[:, 0:1]
    real = jnp.where(valid, orbitals[0, 0], 0.0)
    imag = jnp.where(valid, orbitals[1, 0], 0.0)
    kinetic = (cols[:, 1:2] + offset * offset) * (1.0 / (RADIUS * RADIUS))
    return real, imag, valid, kinetic


def pack(real, imag):
    lane = lax.broadcasted_iota(jnp.int32, real.shape, 1)
    first = lane < 64
    main = jnp.where(first, real, pltpu.roll(imag, 64, 1))
    last = jnp.where(first, pltpu.roll(real, 64, 1), imag)
    last = jnp.where(lane % 64 == 0, last, 0.0)
    return main + jnp.concatenate([last[OWN - 1 :], last[: OWN - 1]], axis=0)


def z_kernel(orb_hbm, high_hbm, low_hbm, coords_hbm, half_hbm, out_ref, left_ref, cols_ref, orb, high, low, coords, half, sems):
    pairs = ((half_hbm, half), (coords_hbm, coords), (orb_hbm, orb), (high_hbm, high), (low_hbm, low))
    copies = [pltpu.make_async_copy(a, b, sems.at[i]) for i, (a, b) in enumerate(pairs)]
    for copy in copies:
        copy.start()
    me = lax.axis_index("zlo") * 2 + lax.axis_index("core")
    tile = jnp.minimum(me * OWN // 128, 25)
    shift = me * OWN - tile * 128
    copies[0].wait()
    copies[1].wait()
    wide = pl.ds(pl.multiple_of(tile * 128, 128), 384)
    own = jnp.concatenate([half[pl.ds(tile + i, 1), :] for i in range(3)], axis=1)
    own = jnp.concatenate([own, coords[:, wide], jnp.zeros((5, 384), jnp.int32)], axis=0).astype(F32)
    own = pltpu.roll(own, lax.rem(384 - shift, 384), 1)[:, :PAD]
    squares = own[1:2] * own[1:2] + own[2:3] * own[2:3]
    cols = jnp.transpose(jnp.concatenate([own[:1], squares, own[2:]], axis=0))
    cols_ref[...] = cols
    copies[2].wait()
    real, imag, _, _ = masked(orb, cols)
    left = pack(real, imag).astype(BF16)
    left_ref[...] = left
    both = jnp.concatenate([real, imag], axis=1)
    both = split(jnp.concatenate([both, jnp.zeros((PAD - OWN, 2 * SLOTS), F32)], axis=0))
    contract = (((1,), (1,)), ((), ()))

    def product(a, b):
        return lax.dot_general(a, b, contract, preferred_element_type=F32)

    copies[3].wait()
    out = product(high[...], both[0]) + product(high[...], both[1])
    copies[4].wait()
    out = out + product(low[...], both[0])
    out_ref[...] = encode(out.reshape(FFT, 2 * PLANES, PAD))


def places(coords_ref, half_ref):
    gx, gy = coords_ref[0:1, :], coords_ref[1:2, :]
    half = jnp.concatenate([half_ref[i : i + 1, :] for i in range(half_ref.shape[0])], axis=1)
    edge = gy == RADIUS
    v = jnp.where(edge, 2 * RADIUS + 1, gx + RADIUS)
    u = jnp.where(edge, 0, gy + RADIUS)
    cell = jnp.where(half >= 0, (v // 4) * 256 + (v % 4) * 64 + u, -256)
    cell = jnp.concatenate([cell, jnp.full((1, PAD - OWN), -256, jnp.int32)], axis=1)
    cell = jnp.concatenate([cell[:, c * OWN : c * OWN + PAD] for c in range(FFT)], axis=0)
    lane = lax.broadcasted_iota(jnp.int32, cell.shape, 1)
    cell = jnp.where(lane < OWN, cell, -256)
    return cell >> 8, cell & 255


def plane_kernel(val_ref, coords_ref, half_ref, pot_ref, yh, yl, xh, xl, bxh, bxl, byh, byl, out_ref, spread_ref, t_ref, g_ref):
    block = 2 * PLANES
    group, col = places(coords_ref, half_ref)
    values = decode(val_ref[...])
    sub = lax.broadcasted_iota(jnp.int32, (256, PAD), 0)
    hots = [jnp.where(sub == col[c : c + 1], 1.0, 0.0).astype(BF16) for c in range(FFT)]
    for c in range(FFT):
        value = values[c]
        high = value.astype(BF16).astype(F32)
        low = value - high
        for r in range(GROUPS):
            here = jnp.broadcast_to(group[c : c + 1] == r, (block, PAD))
            spread_ref[r * block : (r + 1) * block, c * PAD : (c + 1) * PAD] = jnp.where(here, high, 0.0).astype(BF16)
            spread_ref[ROWS + r * block : ROWS + (r + 1) * block, c * PAD : (c + 1) * PAD] = jnp.where(here, low, 0.0).astype(BF16)
    window = lax.dot_general(
        jnp.concatenate(hots, axis=1), spread_ref[...], (((1,), (1,)), ((), ())), preferred_element_type=F32
    )
    window = jnp.transpose(window)
    window = window[:ROWS] + window[ROWS:]

    quarter = lax.broadcasted_iota(jnp.int32, (ROWS, 256), 1) // 64
    stacked = jnp.concatenate([jnp.where(quarter == q, window, 0.0) for q in range(4)], axis=0)
    along = dot3(split(stacked), (yh[...], yl[...]))
    along = along.reshape(4, GROUPS, 2, PLANES, 256)
    real = along[:, :, 0, :, :GRID] - along[:, :, 1, :, GRID:]
    imag = along[:, :, 0, :, GRID:] + along[:, :, 1, :, :GRID]
    parity = lax.broadcasted_iota(jnp.int32, (PLANES, GRID), 1) % 2
    sign = jnp.where(parity == 1, -1.0, 1.0)
    half = 4 * GROUPS * PLANES
    t_ref[:half, :] = real.reshape(half, GRID)
    t_ref[half:, :] = imag.reshape(half, GRID)
    special = (GROUPS + 16) * PLANES
    for base in (special, half + special):
        t_ref[base : base + PLANES, :] = t_ref[base : base + PLANES, :] * sign

    count = 2 * 4 * GROUPS
    fill = jnp.zeros((KX - count, 256), F32)
    for pair in range(PLANES // 2):
        p = 2 * pair
        planes = [t_ref[pl.ds(p + i, count, stride=PLANES), :] for i in range(2)]
        part = jnp.concatenate([jnp.concatenate(planes, axis=1), fill], axis=0)
        field = dot3((xh[...], xl[...]), split(part))
        pot = jnp.concatenate([pot_ref[p], pot_ref[p + 1]], axis=1)
        field = field * jnp.concatenate([pot, pot], axis=0)
        back = dot3((bxh[...], bxl[...]), split(field))
        for i in range(2):
            g_ref[pl.ds(p + i, count, stride=PLANES), :] = back[:count, i * GRID : (i + 1) * GRID]
    for base in (special, half + special):
        g_ref[base : base + PLANES, :] = g_ref[base : base + PLANES, :] * sign

    couple = split(jnp.concatenate([g_ref[:half, :], g_ref[half:, :]], axis=1))
    parts = []
    rows = GROUPS * PLANES
    quarter = lax.broadcasted_iota(jnp.int32, (rows, 256), 1) // 64
    for i in range(2):
        cells = dot3(couple, (byh[i], byl[i]))
        total = cells[:rows]
        for q in range(1, 4):
            total = jnp.where(quarter == q, cells[q * rows : (q + 1) * rows], total)
        parts.append(total.reshape(GROUPS, 1, PLANES, 256))
    cells = jnp.concatenate(parts, axis=1).reshape(ROWS, 256)
    high, low = split(cells)
    cells = jnp.concatenate([high, low], axis=0)

    for c in range(FFT):
        found = dot(cells, hots[c])
        found = found[:ROWS] + found[ROWS:]
        total = jnp.zeros((block, PAD), F32)
        for r in range(GROUPS):
            here = jnp.broadcast_to(group[c : c + 1] == r, (block, PAD))
            total = jnp.where(here, found[r * block : (r + 1) * block], total)
        out_ref[c : c + 1] = encode(total[None])


def apply_kernel(mix_ref, orb_ref, cols_ref, high_ref, low_ref, applied_ref, spread_ref):
    real, imag, valid, kinetic = masked(orb_ref, cols_ref[...])
    mixed = dot3((high_ref[...], low_ref[...]), split(decode(mix_ref[...]).reshape(256, PAD)))
    mixed_real = jnp.transpose(mixed[:SLOTS])[:OWN]
    mixed_imag = jnp.transpose(mixed[SLOTS:])[:OWN]
    applied_real = jnp.where(valid, kinetic * real + mixed_real, 0.0)
    applied_imag = jnp.where(valid, kinetic * imag + mixed_imag, 0.0)
    applied_ref[0, 0] = applied_real
    applied_ref[1, 0] = applied_imag
    right = pack(applied_real, applied_imag).astype(BF16)
    left = pack(real, imag).astype(BF16)
    for i in range(spread_ref.shape[0]):
        spread_ref[i, 0] = right
        spread_ref[i, 1] = left


def block_kernel(left_ref, pair_ref, out_ref, sums_ref, second_ref):
    sides, depth, width = 2, 4, pair_ref.shape[0]
    lane = lax.broadcasted_iota(jnp.int32, (OWN, SLOTS), 1)
    sign = jnp.where(lane < 64, 1.0, -1.0)
    side, y = lax.axis_index("zhi"), lax.axis_index("y")

    def column(x, carry):
        for m in range(2):
            second = pair_ref[x, m].astype(F32)
            second_ref[2 * m] = second
            second_ref[2 * m + 1] = pltpu.roll(second, 64, 1) * sign
        for order in range(depth):
            mine = [left_ref[order * sides + other].astype(F32) for other in range(sides)]
            near = y + (order % 2) * (1 - 2 * lax.rem(y, 2))
            line = depth - 1 - near if order >= 2 else near
            for t in range(4):
                second = second_ref[t]
                for other in range(sides):
                    product = (mine[other] * second).reshape(OWN // 8, 8, SLOTS)
                    row = line + depth * lax.rem(side + other, sides)
                    place = (t * sides * depth + row) * width + x
                    sums_ref[pl.ds(pl.multiple_of(place * 8, 8), 8), :] = jnp.sum(product, axis=0)
        return carry

    lax.fori_loop(0, width, column, 0)
    total = jnp.sum(sums_ref[...].reshape(-1, 8, SLOTS), axis=1)
    ones = jnp.ones((8, SLOTS), F32)
    summed = lax.dot_general(
        ones, total, (((1,), (1,)), ((), ())), precision=lax.Precision.HIGHEST, preferred_element_type=F32
    )
    out_ref[...] = summed * (1.0 / RADIUS**3)


def matrix_kernel(columns_ref, out_ref):
    depth = width = 4
    sides = columns_ref.shape[1]
    lane = lax.broadcasted_iota(jnp.int32, (depth * sides, SLOTS), 1) % width
    rows = []
    for x in range(width):
        rows.append(jnp.concatenate([columns_ref[y * width + x] for y in range(depth)], axis=0))
    bands = []
    for right in range(width):
        merged = rows[right]
        for x in range(width):
            if x != right:
                merged = jnp.where(lane == x, pltpu.roll(rows[x], (x - right) % SLOTS, 1), merged)
        bands.append(merged)
    order = [(side, y, x) for side in range(sides) for y in range(depth) for x in range(width)]
    columns = jnp.concatenate([bands[x][y * sides + side : y * sides + side + 1] for side, y, x in order], axis=0)
    out_ref[...] = jnp.transpose(columns)


def call(kernel, out_shape, count, scratch=(), flops=10**8, traffic=10**6, hbm=(), limit=VMEM):
    return pl.pallas_call(
        kernel,
        out_shape=out_shape,
        in_specs=[pl.BlockSpec(memory_space=pl.ANY if i in hbm else pltpu.VMEM) for i in range(count)],
        scratch_shapes=list(scratch),
        compiler_params=pltpu.CompilerParams(vmem_limit_bytes=limit),
        cost_estimate=pl.CostEstimate(flops=flops, bytes_accessed=traffic, transcendentals=0),
    )


def solution(mesh):
    fft = mesh.shape["fft"]
    sides, depth, width = 2, 4, 4
    fine = Mesh(mesh.devices.reshape(fft // 2, 2, sides, depth, width), FULL)
    groups = depth * width
    bands = sides * groups
    shaped = jax.ShapeDtypeStruct

    zh, zl = halves(z_table())
    yh, yl = halves(y_table())
    xh, xl = halves(x_table())
    byh, byl = halves(y_back_table())

    def local(orbitals, potential, stick_coords, stick_half):
        halves_of = stick_half.reshape(28, 128)
        stick = (OWN, SLOTS)
        sent, left, cols = call(
            z_kernel,
            [shaped((FFT, 2 * PLANES, PAD), jnp.int16), shaped(stick, BF16), shaped((PAD, 8), F32)],
            5,
            scratch=[
                pltpu.VMEM(orbitals.shape, F32),
                pltpu.VMEM(zh.shape, BF16),
                pltpu.VMEM(zl.shape, BF16),
                pltpu.VMEM(stick_coords.shape, jnp.int32),
                pltpu.VMEM((28, 128), jnp.int32),
                pltpu.SemaphoreType.DMA((5,)),
            ],
            flops=5 * 10**10,
            traffic=10**8,
            hbm=range(5),
            limit=WHOLE,
        )(orbitals, zh, zl, stick_coords, halves_of)
        received = lax.all_to_all(sent, ("zlo", "core"), 0, 0, tiled=True)

        picked = call(
            plane_kernel,
            shaped((FFT, 2 * PLANES, PAD), jnp.int16),
            12,
            scratch=[
                pltpu.VMEM((2 * ROWS, FFT * PAD), BF16),
                pltpu.VMEM((2 * 4 * GROUPS * PLANES, GRID), F32),
                pltpu.VMEM((2 * 4 * GROUPS * PLANES, GRID), F32),
            ],
            flops=1,
            traffic=1,
        )(received, stick_coords, halves_of, potential, yh, yl, xh, xl, xh.T, xl.T, byh, byl)

        far = lax.ppermute(left, "zhi", [(0, 1), (1, 0)])
        picked, far = lax.optimization_barrier((picked, far))
        lefts = jnp.stack([left, far])
        beside = lax.ppermute(lefts, "y", [(i, i ^ 1) for i in range(depth)])
        lefts = jnp.concatenate([lefts, beside])
        lefts = jnp.concatenate([lefts, lax.ppermute(lefts, "y", [(i, depth - 1 - i) for i in range(depth)])])

        mixed = lax.all_to_all(picked, ("zlo", "core"), 0, 0, tiled=True)
        applied, spread = call(apply_kernel, [shaped(orbitals.shape, F32), shaped((width, 2) + stick, BF16)], 5)(
            mixed, orbitals, cols, zh.T, zl.T
        )
        pairs = lax.all_to_all(spread, "x", 0, 0, tiled=True)
        column = call(
            block_kernel,
            shaped((8, 4 * bands), F32),
            2,
            scratch=[pltpu.VMEM((4 * bands * 8, SLOTS), F32), pltpu.VMEM((4,) + stick, F32)],
        )(lefts, pairs)
        column = jnp.broadcast_to(column[:1][None], (fft * sides, 1, 4 * bands))
        column = lax.all_to_all(column, ("zlo", "core", "zhi"), 0, 0, tiled=True)
        column = jnp.sum(column.reshape(fft, sides, 4 * bands), axis=0)
        column = jnp.broadcast_to(column[None], (groups, sides, 4 * bands))
        columns = lax.all_to_all(column, ("y", "x"), 0, 0, tiled=True)
        subspace = call(matrix_kernel, shaped((4 * bands, bands), F32), 1)(columns)
        subspace = subspace.reshape(2, 2, bands, bands)
        return applied, subspace

    across = ("zhi", "y", "x")
    along = ("zlo", "core")
    return jax.shard_map(
        local,
        mesh=fine,
        in_specs=(P(None, across, along, None), P(along, None, None), P(), P()),
        out_specs=(P(None, across, along, None), P()),
        check_vma=False,
    )
```

```python
import math

import jax
import jax.numpy as jnp
import ml_dtypes
import numpy as np
from jax import lax
from jax.experimental import pallas as pl
from jax.experimental.pallas import tpu as pltpu
from jax.sharding import Mesh
from jax.sharding import PartitionSpec as P

RADIUS = 32
GRID = 128
SLOTS = 128
FFT = 16
OWN = 224
PAD = 256
LEVELS = 32767.0
PLANES = 8
GROUPS = 17
ROWS = GROUPS * 2 * PLANES
KX = 144
F32 = jnp.float32
BF16 = jnp.bfloat16
FULL = ("zlo", "core", "zhi", "y", "x")
VMEM = 48 * 1024 * 1024
WHOLE = 62 * 1024 * 1024


def halves(table):
    high = table.astype(ml_dtypes.bfloat16)
    low = (table - high.astype(np.float64)).astype(ml_dtypes.bfloat16)
    return high, low


def waves(first, second):
    angle = (np.outer(first, second) % GRID) * (2.0 * math.pi / GRID)
    return np.cos(angle), np.sin(angle)


def z_table():
    cos, sin = waves(np.arange(GRID), np.arange(SLOTS) - RADIUS)
    cos[:, 2 * RADIUS + 1 :] = 0.0
    sin[:, 2 * RADIUS + 1 :] = 0.0
    real = np.concatenate([cos, -sin], axis=1).reshape(FFT, 1, PLANES, 2 * SLOTS)
    imag = np.concatenate([sin, cos], axis=1).reshape(FFT, 1, PLANES, 2 * SLOTS)
    return np.concatenate([real, imag], axis=1).reshape(2 * GRID, 2 * SLOTS)


def y_table():
    cos, sin = waves(np.arange(64) - RADIUS, np.arange(GRID))
    return np.tile(np.concatenate([cos, sin], axis=1), (4, 1))


def x_table():
    v = 4 * np.arange(GROUPS)[None, :] + np.arange(4)[:, None]
    freq = np.where(v <= 2 * RADIUS, v - RADIUS, 0).reshape(-1)
    cos, sin = waves(np.arange(GRID), freq)
    table = np.zeros((2 * GRID, KX))
    table[:GRID, :68], table[:GRID, 68:136] = cos, -sin
    table[GRID:, :68], table[GRID:, 68:136] = sin, cos
    return table


def y_back_table():
    cos, sin = waves(np.arange(GRID), np.arange(64) - RADIUS)
    real = np.concatenate([cos, sin], axis=0)
    imag = np.concatenate([-sin, cos], axis=0)
    return np.stack([np.tile(real, (1, 4)), np.tile(imag, (1, 4))]) * (1.0 / GRID**3)


def split(value):
    high = value.astype(BF16)
    return high, (value - high.astype(F32)).astype(BF16)


def dot(left, right):
    return jnp.dot(left, right, preferred_element_type=F32)


def dot3(left, right):
    return dot(left[0], right[0]) + dot(left[1], right[0]) + dot(left[0], right[1])


def encode(value):
    top = jnp.max(jnp.max(jnp.abs(value), axis=1, keepdims=True), axis=2, keepdims=True)
    power = jnp.floor(jnp.log2(jnp.maximum(top, 1e-36))) + 1.0
    size = jnp.maximum(jnp.abs(value) * jnp.exp2(-power), 1e-30)
    size = jnp.minimum(jnp.exp2(jnp.log2(size) * (1.0 / 3.0)) * LEVELS + 0.5, LEVELS)
    size = jnp.floor(size)
    coded = jnp.where(value < 0.0, -size, size)
    lane = lax.broadcasted_iota(jnp.int32, value.shape, 2)
    return jnp.where(lane == OWN, power, coded).astype(jnp.int32).astype(jnp.int16)


def decode(coded):
    coded = coded.astype(jnp.int32).astype(F32)
    root = coded * (1.0 / LEVELS)
    return root * root * root * jnp.exp2(coded[:, :, OWN : OWN + 1])


def masked(orbitals, cols):
    cols = cols[:OWN]
    offset = lax.broadcasted_iota(jnp.int32, (OWN, SLOTS), 1).astype(F32) - RADIUS
    valid = jnp.abs(offset) <= cols[:, 0:1]
    real = jnp.where(valid, orbitals[0, 0], 0.0)
    imag = jnp.where(valid, orbitals[1, 0], 0.0)
    kinetic = (cols[:, 1:2] + offset * offset) * (1.0 / (RADIUS * RADIUS))
    return real, imag, valid, kinetic


def pack(real, imag):
    lane = lax.broadcasted_iota(jnp.int32, real.shape, 1)
    first = lane < 64
    main = jnp.where(first, real, pltpu.roll(imag, 64, 1))
    last = jnp.where(first, pltpu.roll(real, 64, 1), imag)
    last = jnp.where(lane % 64 == 0, last, 0.0)
    return main + jnp.concatenate([last[OWN - 1 :], last[: OWN - 1]], axis=0)


def z_kernel(orb_hbm, high_hbm, low_hbm, coords_hbm, half_hbm, out_ref, left_ref, cols_ref, orb, high, low, coords, half, sems):
    pairs = ((half_hbm, half), (coords_hbm, coords), (orb_hbm, orb), (high_hbm, high), (low_hbm, low))
    copies = [pltpu.make_async_copy(a, b, sems.at[i]) for i, (a, b) in enumerate(pairs)]
    for copy in copies:
        copy.start()
    me = lax.axis_index("zlo") * 2 + lax.axis_index("core")
    tile = jnp.minimum(me * OWN // 128, 25)
    shift = me * OWN - tile * 128
    copies[0].wait()
    copies[1].wait()
    wide = pl.ds(pl.multiple_of(tile * 128, 128), 384)
    own = jnp.concatenate([half[pl.ds(tile + i, 1), :] for i in range(3)], axis=1)
    own = jnp.concatenate([own, coords[:, wide], jnp.zeros((5, 384), jnp.int32)], axis=0).astype(F32)
    own = pltpu.roll(own, lax.rem(384 - shift, 384), 1)[:, :PAD]
    squares = own[1:2] * own[1:2] + own[2:3] * own[2:3]
    cols = jnp.transpose(jnp.concatenate([own[:1], squares, own[2:]], axis=0))
    cols_ref[...] = cols
    copies[2].wait()
    real, imag, _, _ = masked(orb, cols)
    left = pack(real, imag).astype(BF16)
    left_ref[...] = left
    both = jnp.concatenate([real, imag], axis=1)
    both = split(jnp.concatenate([both, jnp.zeros((PAD - OWN, 2 * SLOTS), F32)], axis=0))
    contract = (((1,), (1,)), ((), ()))

    def product(a, b):
        return lax.dot_general(a, b, contract, preferred_element_type=F32)

    copies[3].wait()
    out = product(high[...], both[0]) + product(high[...], both[1])
    copies[4].wait()
    out = out + product(low[...], both[0])
    out_ref[...] = encode(out.reshape(FFT, 2 * PLANES, PAD))


def places(coords_ref, half_ref):
    gx, gy = coords_ref[0:1, :], coords_ref[1:2, :]
    half = jnp.concatenate([half_ref[i : i + 1, :] for i in range(half_ref.shape[0])], axis=1)
    edge = gy == RADIUS
    v = jnp.where(edge, 2 * RADIUS + 1, gx + RADIUS)
    u = jnp.where(edge, 0, gy + RADIUS)
    cell = jnp.where(half >= 0, (v // 4) * 256 + (v % 4) * 64 + u, -256)
    cell = jnp.concatenate([cell, jnp.full((1, PAD - OWN), -256, jnp.int32)], axis=1)
    cell = jnp.concatenate([cell[:, c * OWN : c * OWN + PAD] for c in range(FFT)], axis=0)
    lane = lax.broadcasted_iota(jnp.int32, cell.shape, 1)
    cell = jnp.where(lane < OWN, cell, -256)
    return cell >> 8, cell & 255


def plane_kernel(val_ref, coords_ref, half_ref, pot_ref, yh, yl, xh, xl, bxh, bxl, byh, byl, out_ref, spread_ref, t_ref, g_ref):
    block = 2 * PLANES
    group, col = places(coords_ref, half_ref)
    values = decode(val_ref[...])
    sub = lax.broadcasted_iota(jnp.int32, (256, PAD), 0)
    hots = [jnp.where(sub == col[c : c + 1], 1.0, 0.0).astype(BF16) for c in range(FFT)]
    for c in range(FFT):
        value = values[c]
        high = value.astype(BF16).astype(F32)
        low = value - high
        for r in range(GROUPS):
            here = jnp.broadcast_to(group[c : c + 1] == r, (block, PAD))
            spread_ref[r * block : (r + 1) * block, c * PAD : (c + 1) * PAD] = jnp.where(here, high, 0.0).astype(BF16)
            spread_ref[ROWS + r * block : ROWS + (r + 1) * block, c * PAD : (c + 1) * PAD] = jnp.where(here, low, 0.0).astype(BF16)
    window = lax.dot_general(
        jnp.concatenate(hots, axis=1), spread_ref[...], (((1,), (1,)), ((), ())), preferred_element_type=F32
    )
    window = jnp.transpose(window)
    window = window[:ROWS] + window[ROWS:]

    quarter = lax.broadcasted_iota(jnp.int32, (ROWS, 256), 1) // 64
    stacked = jnp.concatenate([jnp.where(quarter == q, window, 0.0) for q in range(4)], axis=0)
    along = dot3(split(stacked), (yh[...], yl[...]))
    along = along.reshape(4, GROUPS, 2, PLANES, 256)
    real = along[:, :, 0, :, :GRID] - along[:, :, 1, :, GRID:]
    imag = along[:, :, 0, :, GRID:] + along[:, :, 1, :, :GRID]
    parity = lax.broadcasted_iota(jnp.int32, (PLANES, GRID), 1) % 2
    sign = jnp.where(parity == 1, -1.0, 1.0)
    half = 4 * GROUPS * PLANES
    t_ref[:half, :] = real.reshape(half, GRID)
    t_ref[half:, :] = imag.reshape(half, GRID)
    special = (GROUPS + 16) * PLANES
    for base in (special, half + special):
        t_ref[base : base + PLANES, :] = t_ref[base : base + PLANES, :] * sign

    count = 2 * 4 * GROUPS
    fill = jnp.zeros((KX - count, 256), F32)
    for pair in range(PLANES // 2):
        p = 2 * pair
        planes = [t_ref[pl.ds(p + i, count, stride=PLANES), :] for i in range(2)]
        part = jnp.concatenate([jnp.concatenate(planes, axis=1), fill], axis=0)
        field = dot3((xh[...], xl[...]), split(part))
        pot = jnp.concatenate([pot_ref[p], pot_ref[p + 1]], axis=1)
        field = field * jnp.concatenate([pot, pot], axis=0)
        back = dot3((bxh[...], bxl[...]), split(field))
        for i in range(2):
            g_ref[pl.ds(p + i, count, stride=PLANES), :] = back[:count, i * GRID : (i + 1) * GRID]
    for base in (special, half + special):
        g_ref[base : base + PLANES, :] = g_ref[base : base + PLANES, :] * sign

    couple = split(jnp.concatenate([g_ref[:half, :], g_ref[half:, :]], axis=1))
    parts = []
    rows = GROUPS * PLANES
    quarter = lax.broadcasted_iota(jnp.int32, (rows, 256), 1) // 64
    for i in range(2):
        cells = dot3(couple, (byh[i], byl[i]))
        total = cells[:rows]
        for q in range(1, 4):
            total = jnp.where(quarter == q, cells[q * rows : (q + 1) * rows], total)
        parts.append(total.reshape(GROUPS, 1, PLANES, 256))
    cells = jnp.concatenate(parts, axis=1).reshape(ROWS, 256)
    high, low = split(cells)
    cells = jnp.concatenate([high, low], axis=0)

    for c in range(FFT):
        found = dot(cells, hots[c])
        found = found[:ROWS] + found[ROWS:]
        total = jnp.zeros((block, PAD), F32)
        for r in range(GROUPS):
            here = jnp.broadcast_to(group[c : c + 1] == r, (block, PAD))
            total = jnp.where(here, found[r * block : (r + 1) * block], total)
        out_ref[c : c + 1] = encode(total[None])


def apply_kernel(mix_ref, orb_ref, left_ref, cols_ref, high_ref, low_ref, applied_ref, spread_ref):
    real, imag, valid, kinetic = masked(orb_ref, cols_ref[...])
    mixed = dot3((high_ref[...], low_ref[...]), split(decode(mix_ref[...]).reshape(256, PAD)))
    mixed_real = jnp.transpose(mixed[:SLOTS])[:OWN]
    mixed_imag = jnp.transpose(mixed[SLOTS:])[:OWN]
    applied_real = jnp.where(valid, kinetic * real + mixed_real, 0.0)
    applied_imag = jnp.where(valid, kinetic * imag + mixed_imag, 0.0)
    applied_ref[0, 0] = applied_real
    applied_ref[1, 0] = applied_imag
    right = pack(applied_real, applied_imag).astype(BF16)
    left = left_ref[...]
    for i in range(spread_ref.shape[0]):
        spread_ref[i, 0] = right
        spread_ref[i, 1] = left


def block_kernel(left_ref, pair_ref, out_ref, sums_ref, second_ref):
    sides, depth, width = 2, 4, pair_ref.shape[0]
    lane = lax.broadcasted_iota(jnp.int32, (OWN, SLOTS), 1)
    sign = jnp.where(lane < 64, 1.0, -1.0)
    side, y = lax.axis_index("zhi"), lax.axis_index("y")

    def column(x, carry):
        for m in range(2):
            second = pair_ref[x, m].astype(F32)
            second_ref[2 * m] = second
            second_ref[2 * m + 1] = pltpu.roll(second, 64, 1) * sign
        for order in range(depth):
            mine = [left_ref[order * sides + other].astype(F32) for other in range(sides)]
            near = y + (order % 2) * (1 - 2 * lax.rem(y, 2))
            line = depth - 1 - near if order >= 2 else near
            for t in range(4):
                second = second_ref[t]
                for other in range(sides):
                    product = (mine[other] * second).reshape(OWN // 8, 8, SLOTS)
                    row = line + depth * lax.rem(side + other, sides)
                    place = (t * sides * depth + row) * width + x
                    sums_ref[pl.ds(pl.multiple_of(place * 8, 8), 8), :] = jnp.sum(product, axis=0)
        return carry

    lax.fori_loop(0, width, column, 0)
    total = jnp.sum(sums_ref[...].reshape(-1, 8, SLOTS), axis=1)
    ones = jnp.ones((8, SLOTS), F32)
    summed = lax.dot_general(
        ones, total, (((1,), (1,)), ((), ())), precision=lax.Precision.HIGHEST, preferred_element_type=F32
    )
    out_ref[...] = summed * (1.0 / RADIUS**3)


def matrix_kernel(columns_ref, out_ref):
    depth = width = 4
    sides = columns_ref.shape[1]
    lane = lax.broadcasted_iota(jnp.int32, (depth * sides, SLOTS), 1) % width
    rows = []
    for x in range(width):
        rows.append(jnp.concatenate([columns_ref[y * width + x] for y in range(depth)], axis=0))
    bands = []
    for right in range(width):
        merged = rows[right]
        for x in range(width):
            if x != right:
                merged = jnp.where(lane == x, pltpu.roll(rows[x], (x - right) % SLOTS, 1), merged)
        bands.append(merged)
    order = [(side, y, x) for side in range(sides) for y in range(depth) for x in range(width)]
    columns = jnp.concatenate([bands[x][y * sides + side : y * sides + side + 1] for side, y, x in order], axis=0)
    out_ref[...] = jnp.transpose(columns)


def call(kernel, out_shape, count, scratch=(), flops=10**8, traffic=10**6, hbm=(), limit=VMEM):
    return pl.pallas_call(
        kernel,
        out_shape=out_shape,
        in_specs=[pl.BlockSpec(memory_space=pl.ANY if i in hbm else pltpu.VMEM) for i in range(count)],
        scratch_shapes=list(scratch),
        compiler_params=pltpu.CompilerParams(vmem_limit_bytes=limit),
        cost_estimate=pl.CostEstimate(flops=flops, bytes_accessed=traffic, transcendentals=0),
    )


def solution(mesh):
    fft = mesh.shape["fft"]
    sides, depth, width = 2, 4, 4
    fine = Mesh(mesh.devices.reshape(fft // 2, 2, sides, depth, width), FULL)
    groups = depth * width
    bands = sides * groups
    shaped = jax.ShapeDtypeStruct

    zh, zl = halves(z_table())
    yh, yl = halves(y_table())
    xh, xl = halves(x_table())
    byh, byl = halves(y_back_table())

    def local(orbitals, potential, stick_coords, stick_half):
        halves_of = stick_half.reshape(28, 128)
        stick = (OWN, SLOTS)
        sent, left, cols = call(
            z_kernel,
            [shaped((FFT, 2 * PLANES, PAD), jnp.int16), shaped(stick, BF16), shaped((PAD, 8), F32)],
            5,
            scratch=[
                pltpu.VMEM(orbitals.shape, F32),
                pltpu.VMEM(zh.shape, BF16),
                pltpu.VMEM(zl.shape, BF16),
                pltpu.VMEM(stick_coords.shape, jnp.int32),
                pltpu.VMEM((28, 128), jnp.int32),
                pltpu.SemaphoreType.DMA((5,)),
            ],
            flops=5 * 10**10,
            traffic=10**8,
            hbm=range(5),
            limit=WHOLE,
        )(orbitals, zh, zl, stick_coords, halves_of)
        received = lax.all_to_all(sent, ("zlo", "core"), 0, 0, tiled=True)

        picked = call(
            plane_kernel,
            shaped((FFT, 2 * PLANES, PAD), jnp.int16),
            12,
            scratch=[
                pltpu.VMEM((2 * ROWS, FFT * PAD), BF16),
                pltpu.VMEM((2 * 4 * GROUPS * PLANES, GRID), F32),
                pltpu.VMEM((2 * 4 * GROUPS * PLANES, GRID), F32),
            ],
            flops=1,
            traffic=1,
        )(received, stick_coords, halves_of, potential, yh, yl, xh, xl, xh.T, xl.T, byh, byl)

        far = lax.ppermute(left, "zhi", [(0, 1), (1, 0)])
        picked, far = lax.optimization_barrier((picked, far))
        lefts = jnp.stack([left, far])
        beside = lax.ppermute(lefts, "y", [(i, i ^ 1) for i in range(depth)])
        lefts = jnp.concatenate([lefts, beside])
        lefts = jnp.concatenate([lefts, lax.ppermute(lefts, "y", [(i, depth - 1 - i) for i in range(depth)])])

        mixed = lax.all_to_all(picked, ("zlo", "core"), 0, 0, tiled=True)
        applied, spread = call(apply_kernel, [shaped(orbitals.shape, F32), shaped((width, 2) + stick, BF16)], 6)(
            mixed, orbitals, left, cols, zh.T, zl.T
        )
        pairs = lax.all_to_all(spread, "x", 0, 0, tiled=True)
        column = call(
            block_kernel,
            shaped((8, 4 * bands), F32),
            2,
            scratch=[pltpu.VMEM((4 * bands * 8, SLOTS), F32), pltpu.VMEM((4,) + stick, F32)],
        )(lefts, pairs)
        column = jnp.broadcast_to(column[:1][None], (fft * sides, 1, 4 * bands))
        column = lax.all_to_all(column, ("zlo", "core", "zhi"), 0, 0, tiled=True)
        column = jnp.sum(column.reshape(fft, sides, 4 * bands), axis=0)
        column = jnp.broadcast_to(column[None], (groups, sides, 4 * bands))
        columns = lax.all_to_all(column, ("y", "x"), 0, 0, tiled=True)
        subspace = call(matrix_kernel, shaped((4 * bands, bands), F32), 1)(columns)
        subspace = subspace.reshape(2, 2, bands, bands)
        return applied, subspace

    across = ("zhi", "y", "x")
    along = ("zlo", "core")
    return jax.shard_map(
        local,
        mesh=fine,
        in_specs=(P(None, across, along, None), P(along, None, None), P(), P()),
        out_specs=(P(None, across, along, None), P()),
        check_vma=False,
    )
```
